32 devices in a mesh: dp: 16 (over z, y, core), tensor: 2 (over x).
Axes of the slice: x: 2, y: 2, z: 4, core: 2. Of those that a mesh axis runs over, the one named last changes fastest.
Arguments:
- tokens: bfloat16 [24576, 640], P('dp'), may hold values from -6 to 6
- w_query: bfloat16 [640, 1024], P(None, 'tensor'), may hold values from -0.25 to 0.25
- w_key: bfloat16 [640, 256], replicated, may hold values from -0.25 to 0.25
- w_value: bfloat16 [640, 256], replicated, may hold values from -0.25 to 0.25
- w_output: bfloat16 [1024, 640], P('tensor'), may hold values from -0.1875 to 0.1875
- w_gate: bfloat16 [640, 2048], P(None, 'tensor'), may hold values from -0.25 to 0.25
- w_up: bfloat16 [640, 2048], P(None, 'tensor'), may hold values from -0.25 to 0.25
- w_down: bfloat16 [2048, 640], P('tensor'), may hold values from -0.125 to 0.125
- gain_input: float32 [640], replicated, may hold values from -0.4 to 0.6
- gain_query: float32 [256], replicated, may hold values from -0.4 to 0.6
- gain_key: float32 [256], replicated, may hold values from -0.4 to 0.6
- gain_post_attn: float32 [640], replicated, may hold values from -0.4 to 0.6
- gain_pre_ffn: float32 [640], replicated, may hold values from -0.4 to 0.6
- gain_post_ffn: float32 [640], replicated, may hold values from -0.4 to 0.6
- out_grad: bfloat16 [24576, 640], P('dp'), may hold values from -6 to 6
- lengths: int32 [24], replicated, may hold values from 1 to 1536, as said below
- holder: int32 [24], replicated, may hold values from 0 to 15
Outputs:
- layer_out: float32 [24576, 640], P('dp')
- tokens_grad: float32 [24576, 640], P('dp')
- grad_w_query: float32 [640, 1024], P(None, 'tensor')
- grad_w_key: float32 [640, 256], replicated
- grad_w_value: float32 [640, 256], replicated
- grad_w_output: float32 [1024, 640], P('tensor')
- grad_w_gate: float32 [640, 2048], P(None, 'tensor')
- grad_w_up: float32 [640, 2048], P(None, 'tensor')
- grad_w_down: float32 [2048, 640], P('tensor')
- grad_gain_input: float32 [640], replicated
- grad_gain_query: float32 [256], replicated
- grad_gain_key: float32 [256], replicated
- grad_gain_post_attn: float32 [640], replicated
- grad_gain_pre_ffn: float32 [640], replicated
- grad_gain_post_ffn: float32 [640], replicated
The draws below stay inside these ranges and needn't reach their ends.
Inputs may be any that keep to these rules, and one draw needn't show every extreme that they name: The sequences of one index d of dp (holder = d) have lengths summing to at most 1536; one sequence has exactly 1536 tokens; an index of dp holds 0 to 3 sequences.
All inputs are finite; a program needn't handle non-finite values.
Results may differ from the reference program's by a relative error of at most 0.015.
Values sent between devices are 32-bit elements; how exact they have to be, the bound alone decides.
A program may use at most 192 MiB of HBM per device.

```python
import jax
import jax.numpy as jnp
from jax import lax

D = 640
HEADS = 4
HD = 256
FF = 2048
TOK_DEV = 1536
TOKENS = 24576
SEQS = 24
N_DP = 16


def make_sequences(key):
    base = jax.random.fold_in(key, 7)
    first_key, second_key, third_key = jax.random.split(base, 3)
    pattern = (jnp.arange(N_DP, dtype=jnp.int32) % 4).astype(jnp.int32)
    counts = jax.random.permutation(first_key, pattern).astype(jnp.int32)
    owners = jnp.repeat(jnp.arange(N_DP, dtype=jnp.int32), counts, total_repeat_length=SEQS).astype(jnp.int32)
    per_device = jnp.repeat(counts, counts, total_repeat_length=SEQS).astype(jnp.int32)
    per_device = jnp.maximum(per_device, 1)
    lowest = (TOK_DEV // (2 * per_device)).astype(jnp.int32)
    highest = (TOK_DEV // per_device).astype(jnp.int32)
    drawn = jax.random.randint(second_key, (SEQS,), lowest, highest + 1).astype(jnp.int32)
    single = jnp.argmax((per_device == 1).astype(jnp.int32)).astype(jnp.int32)
    drawn = jnp.where(jnp.arange(SEQS, dtype=jnp.int32) == single, TOK_DEV, drawn).astype(jnp.int32)
    order = jax.random.permutation(third_key, SEQS)
    return (drawn[order], owners[order])


def draw_lengths(key, part):
    return make_sequences(key)[0]


def draw_holder(key, part):
    return make_sequences(key)[1]


def level_of(key, extent, pieces, low, high):
    factor_of = 1.0
    for dim, shards_of in pieces:
        heights = jax.random.uniform(jax.random.fold_in(jax.random.fold_in(key, 6), dim), (shards_of,), jnp.float32, low / len(pieces), high / len(pieces))
        factor_of = factor_of * jnp.repeat(jnp.exp(heights), extent[dim] // shards_of).reshape((-1,) + (1,) * (len(extent) - 1 - dim))
    return factor_of


def normal_values(own_key, shape, width, bound, pieces=(), kind=jnp.bfloat16):
    entries = jax.random.normal(own_key, shape, jnp.float32) * width
    if len(pieces) > 0:
        entries = level_of(own_key, shape, pieces, -0.22, 0.18) * entries
    return jnp.clip(entries, min=-bound, max=bound).astype(kind)


def setup_inputs(seed: int = 0) -> dict:
    seeds = jax.random.split(jax.random.key(seed), 18)
    return {
        "tokens": normal_values(seeds[0], (TOKENS, D), 1.0, 6.0, ((0, 16),)),
        "w_query": normal_values(seeds[1], (D, HEADS * HD), D ** -0.5, 0.25, ((1, 2),)),
        "w_key": normal_values(seeds[2], (D, HD), D ** -0.5, 0.25),
        "w_value": normal_values(seeds[3], (D, HD), D ** -0.5, 0.25),
        "w_output": normal_values(seeds[4], (HEADS * HD, D), (HEADS * HD) ** -0.5, 0.1875, ((0, 2),)),
        "w_gate": normal_values(seeds[5], (D, FF), D ** -0.5, 0.25, ((1, 2),)),
        "w_up": normal_values(seeds[6], (D, FF), D ** -0.5, 0.25, ((1, 2),)),
        "w_down": normal_values(seeds[7], (FF, D), FF ** -0.5, 0.125, ((0, 2),)),
        "gain_input": jnp.clip(jax.random.uniform(seeds[8], (D,), jnp.float32, -0.4, 0.6), -0.4, 0.6),
        "gain_query": jnp.clip(jax.random.uniform(seeds[9], (HD,), jnp.float32, -0.4, 0.6), -0.4, 0.6),
        "gain_key": jnp.clip(jax.random.uniform(seeds[10], (HD,), jnp.float32, -0.4, 0.6), -0.4, 0.6),
        "gain_post_attn": jnp.clip(jax.random.uniform(seeds[11], (D,), jnp.float32, -0.4, 0.6), -0.4, 0.6),
        "gain_pre_ffn": jnp.clip(jax.random.uniform(seeds[12], (D,), jnp.float32, -0.4, 0.6), -0.4, 0.6),
        "gain_post_ffn": jnp.clip(jax.random.uniform(seeds[13], (D,), jnp.float32, -0.4, 0.6), -0.4, 0.6),
        "out_grad": normal_values(seeds[14], (TOKENS, D), 1.0, 6.0, ((0, 16),)),
        "lengths": draw_lengths(jax.random.fold_in(seeds[17], 71), 0),
        "holder": draw_holder(jax.random.fold_in(seeds[17], 71), 0),
    }


EPS = 1e-06
THETA = 1000000.0
HIGH = lax.Precision.HIGHEST

@jax.custom_vjp
def low(v):
    return lax.optimization_barrier(v.astype(jnp.bfloat16)).astype(jnp.float32)

@jax.custom_vjp
def low_back(v):
    return v

def low_keep(v):
    return (low(v), None)

def low_pass(kept, grad):
    return (grad,)

def back_keep(v):
    return (v, None)

def back_low(kept, grad):
    return (low(grad),)
low.defvjp(low_keep, low_pass)
low_back.defvjp(back_keep, back_low)

def layout(lengths, holder, device, tok_rows):
    seq_count = lengths.shape[0]
    owned_mask = holder == device
    local_len = jnp.where(owned_mask, lengths, 0).astype(jnp.int32)
    starts = (jnp.cumsum(local_len) - local_len).astype(jnp.int32)
    row_ids = jnp.arange(tok_rows, dtype=jnp.int32)[:, None]
    inside = owned_mask[None, :] & (row_ids >= starts[None, :]) & (row_ids < (starts + local_len)[None, :])
    inside_int = inside.astype(jnp.int32)
    segment = lax.optimization_barrier(jnp.sum(inside_int * (jnp.arange(seq_count, dtype=jnp.int32)[None, :] + 1), axis=1)) - 1
    position = lax.optimization_barrier(jnp.sum(inside_int * (row_ids - starts[None, :]), axis=1))
    return (segment.astype(jnp.int32), position.astype(jnp.int32))

def rotary_tables(position):
    half_width = HD // 2
    frequency = THETA ** (-(2.0 * jnp.arange(half_width, dtype=jnp.float32)) / HD)
    angles = position.astype(jnp.float32)[:, None] * frequency[None, :]
    angles = jnp.concatenate([angles, angles], axis=1)
    return (jnp.cos(angles), jnp.sin(angles))

def rotate(vectors, cosine, sine):
    half_width = vectors.shape[-1] // 2
    turned = jnp.concatenate([-vectors[..., half_width:], vectors[..., :half_width]], axis=-1)
    return vectors * cosine + turned * sine

def rms_norm(vectors, scaling):
    return vectors * lax.rsqrt(lax.optimization_barrier(jnp.mean(vectors * vectors, axis=-1, keepdims=True)) + EPS) * (1.0 + scaling)

def attention(query_states, key_states, value_states, segment):
    block_rows = min(512, TOK_DEV)
    block_count = TOK_DEV // block_rows
    query_blocks = query_states.reshape(block_count, block_rows, HEADS, HD)
    first_rows = jnp.arange(block_count, dtype=jnp.int32) * block_rows
    column_ids = jnp.arange(TOK_DEV, dtype=jnp.int32)

    def one_block(inputs):
        query_block, first_row = inputs
        row_ids = first_row + jnp.arange(block_rows, dtype=jnp.int32)
        seg_rows = lax.dynamic_slice_in_dim(segment, first_row, block_rows)
        allowed = (seg_rows[:, None] == segment[None, :]) & (seg_rows[:, None] >= 0) & (column_ids[None, :] <= row_ids[:, None]) | (column_ids[None, :] == row_ids[:, None])
        scores = low_back(jnp.einsum('qhd,kd->hqk', query_block, key_states, precision=HIGH)) * HD ** (-0.5)
        scores = jnp.where(allowed[None, :, :], scores, -1e+30)
        row_max = lax.optimization_barrier(jnp.max(scores, axis=-1, keepdims=True))
        exponent = jnp.exp(scores - row_max)
        attn_probs = exponent / lax.optimization_barrier(jnp.sum(exponent, axis=-1, keepdims=True))
        return jnp.einsum('hqk,kd->qhd', low(attn_probs), value_states, precision=HIGH)
    result = lax.map(jax.checkpoint(one_block), (query_blocks, first_rows))
    return result.reshape(TOK_DEV, HEADS, HD)

def layer(inputs_f, w_query, w_key, w_value, w_output, w_gate, w_up, w_down, gain_input, gain_query, gain_key, gain_post_attn, gain_pre_ffn, gain_post_ffn, segment, cosine, sine):
    normed = low(rms_norm(inputs_f, gain_input))
    query_pre = low_back(jnp.dot(normed, w_query, precision=HIGH)).reshape(TOK_DEV, HEADS, HD)
    key_pre = jnp.dot(normed, w_key, precision=HIGH)
    value_pre = jnp.dot(normed, w_value, precision=HIGH)
    query_states = low(rotate(rms_norm(query_pre, gain_query), cosine[:, None, :], sine[:, None, :]))
    key_states = low(rotate(rms_norm(key_pre, gain_key), cosine, sine))
    value_states = low(value_pre)
    mixed_heads = low(low_back(attention(query_states, key_states, value_states, segment))).reshape(TOK_DEV, HEADS * HD)
    branch = low_back(jnp.dot(mixed_heads, w_output, precision=HIGH))
    middle = inputs_f + rms_norm(branch, gain_post_attn)
    normed2 = low(rms_norm(middle, gain_pre_ffn))
    gate_proj = low_back(jnp.dot(normed2, w_gate, precision=HIGH))
    up_proj = low_back(jnp.dot(normed2, w_up, precision=HIGH))
    hidden = low(jax.nn.gelu(gate_proj, approximate=True) * up_proj)
    ffn_sum = low_back(jnp.dot(hidden, w_down, precision=HIGH))
    return middle + rms_norm(ffn_sum, gain_post_ffn)

def reference(tokens, w_query, w_key, w_value, w_output, w_gate, w_up, w_down, gain_input, gain_query, gain_key, gain_post_attn, gain_pre_ffn, gain_post_ffn, out_grad, lengths, holder):
    weights = tuple((matrix.astype(jnp.float32) for matrix in (w_query, w_key, w_value, w_output, w_gate, w_up, w_down, gain_input, gain_query, gain_key, gain_post_attn, gain_pre_ffn, gain_post_ffn)))
    input_rows = tokens.astype(jnp.float32).reshape(N_DP, TOK_DEV, D)
    cotangents = out_grad.astype(jnp.float32).reshape(N_DP, TOK_DEV, D)

    def device_step(sums_carry, inputs):
        rows_dev, cot_dev, device = inputs
        segment, position = layout(lengths, holder, device, TOK_DEV)
        cosine, sine = rotary_tables(position)

        def forward(inputs_f, *params):
            return layer(inputs_f, *params, segment, cosine, sine)
        result, pullback = jax.vjp(forward, rows_dev, *weights)
        valid = (segment >= 0).astype(jnp.float32)[:, None]
        gradients = pullback(cot_dev * valid)
        sums_carry = tuple((summand + addend for summand, addend in zip(sums_carry, gradients[1:])))
        return (sums_carry, (result, gradients[0]))
    zeroes = tuple((jnp.zeros_like(matrix) for matrix in weights))
    totals, (outputs, input_grads) = lax.scan(device_step, zeroes, (input_rows, cotangents, jnp.arange(N_DP, dtype=jnp.int32)))
    return (outputs.reshape(N_DP * TOK_DEV, D), input_grads.reshape(N_DP * TOK_DEV, D), totals[0], totals[1], totals[2], totals[3], totals[4], totals[5], totals[6], totals[7], totals[8], totals[9], totals[10], totals[11], totals[12])
```

```python
import jax
import jax.numpy as jnp
from jax import lax
from jax.experimental import pallas as pl
from jax.experimental.pallas import tpu as pltpu
from jax.sharding import PartitionSpec as P

HD = 256


EPS = 1e-06
THETA = 1000000.0


def layout(lengths, holder, device, tok_rows):
    seq_count = lengths.shape[0]
    owned_mask = holder == device
    local_len = jnp.where(owned_mask, lengths, 0)
    ids = jnp.arange(seq_count, dtype=jnp.int32)
    starts = jnp.sum(jnp.where(ids[:, None] < ids[None, :], local_len[:, None], 0), axis=0)
    row_ids = jnp.arange(tok_rows, dtype=jnp.int32)[:, None]
    inside = (
        owned_mask[None, :]
        & (row_ids >= starts[None, :])
        & (row_ids < (starts + local_len)[None, :])
    )
    reached = jnp.sum(jnp.where(inside, row_ids - starts[None, :] + 1, 0), axis=1)
    return (reached > 0, jnp.maximum(reached - 1, 0))


def rotary_tables(position):
    half_width = HD // 2
    frequency = THETA ** (-(2.0 * jnp.arange(half_width, dtype=jnp.float32)) / HD)
    angles = position.astype(jnp.float32)[:, None] * frequency[None, :]
    return (jnp.cos(angles), jnp.sin(angles))


def rotate(vectors, cosine, sine):
    half_width = HD // 2
    first, second = vectors[:, :half_width], vectors[:, half_width:]
    return jnp.concatenate(
        [first * cosine - second * sine, second * cosine + first * sine], axis=1
    )


def unrotate(grads_in, cosine, sine):
    half_width = HD // 2
    first, second = grads_in[:, :half_width], grads_in[:, half_width:]
    return jnp.concatenate(
        [first * cosine + second * sine, second * cosine - first * sine], axis=1
    )


def norm_forward(vectors, scaling):
    inverse = lax.rsqrt(jnp.mean(vectors * vectors, axis=-1, keepdims=True) + EPS)
    plain = vectors * inverse
    return (plain * (1.0 + scaling), plain, inverse)


def norm_backward(grads_in, plain, inverse, scaling):
    scaled = grads_in * (1.0 + scaling)
    grads_out = inverse * (scaled - plain * jnp.mean(scaled * plain, axis=-1, keepdims=True))
    gain_grad = jnp.sum(grads_in * plain, axis=0)
    return (grads_out, gain_grad)


def dot(first, second):
    return jnp.dot(first, second, preferred_element_type=jnp.float32)


def left_dot(first, second):
    return lax.dot_general(
        first, second, (((0,), (0,)), ((), ())), preferred_element_type=jnp.float32
    )


def right_dot(first, second):
    return lax.dot_general(
        first, second, (((1,), (1,)), ((), ())), preferred_element_type=jnp.float32
    )


def gelu_tanh(vectors):
    return jax.nn.gelu(vectors, approximate=True)


def softmax_rows(row_ref, low_ref, query, keys):
    scores = right_dot(query, keys) * (HD ** (-0.5))
    column_ids = lax.broadcasted_iota(jnp.int32, scores.shape, 1)
    allowed = (column_ids <= row_ref[...]) & (column_ids >= low_ref[...])
    scores = jnp.where(allowed, scores, -1e30)
    exponent = jnp.exp(scores - jnp.max(scores, axis=1, keepdims=True))
    return exponent * (1.0 / jnp.sum(exponent, axis=1, keepdims=True))


def attend_kernel(row_ref, low_ref, query_ref, key_ref, value_ref, mixed_ref):
    probs = softmax_rows(row_ref, low_ref, query_ref[...], key_ref[...])
    mixed_ref[...] = dot(probs.astype(jnp.bfloat16), value_ref[...]).astype(jnp.bfloat16)


def attend_back_kernel(
    row_ref, low_ref, query_ref, key_ref, value_ref, grad_ref, query_grad_ref, key_sum, value_sum
):
    @pl.when(pl.program_id(0) == 0)
    def _():
        key_sum[...] = jnp.zeros_like(key_sum)
        value_sum[...] = jnp.zeros_like(value_sum)

    query, keys, grads_in = query_ref[...], key_ref[...], grad_ref[...]
    probs = softmax_rows(row_ref, low_ref, query, keys)
    value_sum[...] += left_dot(probs.astype(jnp.bfloat16), grads_in)
    grad_probs = right_dot(grads_in, value_ref[...])
    inner = jnp.sum(probs * grad_probs, axis=1, keepdims=True)
    grad_scores = (probs * (grad_probs - inner) * (HD ** (-0.5))).astype(jnp.bfloat16)
    query_grad_ref[...] = dot(grad_scores, keys)
    key_sum[...] += left_dot(grad_scores, query)


def attention_specs(block_rows, key_rows):
    column = pl.BlockSpec((block_rows, 1), lambda h: (0, 0))
    head = pl.BlockSpec((block_rows, HD), lambda h: (0, h))
    keys = pl.BlockSpec((key_rows, HD), lambda h: (0, 0))
    return column, head, keys


def attend(rows, lows, queries, keys, values, key_rows):
    block_rows, width = queries.shape
    heads = width // HD
    column, head, whole = attention_specs(block_rows, key_rows)
    work = block_rows * key_rows * heads
    return pl.pallas_call(
        attend_kernel,
        grid=(heads,),
        out_shape=jax.ShapeDtypeStruct(queries.shape, jnp.bfloat16),
        in_specs=[column, column, head, whole, whole],
        out_specs=head,
        compiler_params=pltpu.CompilerParams(vmem_limit_bytes=40 * 2**20),
        cost_estimate=pl.CostEstimate(
            flops=4 * work * HD, bytes_accessed=4 * 2**20, transcendentals=work
        ),
    )(rows, lows, queries, keys, values)


def attend_back(rows, lows, queries, keys, values, grads_in, key_rows):
    block_rows, width = queries.shape
    heads = width // HD
    column, head, whole = attention_specs(block_rows, key_rows)
    work = block_rows * key_rows * heads
    sums = jax.ShapeDtypeStruct((key_rows, HD), jnp.float32)
    return pl.pallas_call(
        attend_back_kernel,
        grid=(heads,),
        out_shape=(jax.ShapeDtypeStruct(queries.shape, jnp.float32), sums, sums),
        in_specs=[column, column, head, whole, whole, head],
        out_specs=(head, whole, whole),
        compiler_params=pltpu.CompilerParams(vmem_limit_bytes=48 * 2**20),
        cost_estimate=pl.CostEstimate(
            flops=10 * work * HD, bytes_accessed=8 * 2**20, transcendentals=work
        ),
    )(rows, lows, queries, keys, values, grads_in)


def across(array):
    return lax.ppermute(array, "tensor", [(0, 1), (1, 0)])


def swap(array, mask):
    size = lax.axis_size("dp")
    return lax.ppermute(array, "dp", [(i, i ^ mask) for i in range(size)])


def bit_of(mask):
    return (lax.axis_index("dp") // mask) % 2


def halve(array, mask):
    half = array.shape[0] // 2
    bit = bit_of(mask)
    sent = lax.dynamic_slice_in_dim(array, (1 - bit) * half, half)
    kept = lax.dynamic_slice_in_dim(array, bit * half, half)
    return kept + swap(sent, mask)


def join(array, mask):
    other = swap(array, mask)
    return jnp.where(
        bit_of(mask) == 0,
        jnp.concatenate([array, other], axis=0),
        jnp.concatenate([other, array], axis=0),
    )


def outer_masks():
    size = lax.axis_size("dp")
    masks, mask = [], 2
    while mask < size:
        masks.append(mask)
        mask *= 2
    return masks


def scatter_sum(mine, theirs):
    crossing = across(halve(theirs, 1))
    total = halve(mine, 1) + crossing
    for mask in outer_masks():
        total = halve(total, mask)
    return total


def spread(total):
    for mask in reversed(outer_masks()):
        total = join(total, mask)
    return join(total, 1)


def fetch(weight, one):
    half = weight.shape[0] // 2
    part = lax.dynamic_slice_in_dim(weight, bit_of(1) * half, half).astype(jnp.float32)
    theirs = join(across(part * one), 1)
    return (theirs * one).astype(jnp.bfloat16)


def local(
    tokens,
    w_query,
    w_key,
    w_value,
    w_output,
    w_gate,
    w_up,
    w_down,
    gain_input,
    gain_query,
    gain_key,
    gain_post_attn,
    gain_pre_ffn,
    gain_post_ffn,
    out_grad,
    lengths,
    holder,
):
    tok_rows, width = tokens.shape
    quarter = tok_rows // 4
    half_rows = tok_rows // 2
    device = lax.axis_index("dp")
    side = lax.axis_index("tensor")
    early, late = side * quarter, (3 - side) * quarter

    def own(array):
        return jnp.concatenate(
            [
                lax.dynamic_slice_in_dim(array, early, quarter),
                lax.dynamic_slice_in_dim(array, late, quarter),
            ],
            axis=0,
        )

    def others(array):
        return jnp.concatenate(
            [
                lax.dynamic_slice_in_dim(array, (1 - side) * quarter, quarter),
                lax.dynamic_slice_in_dim(array, (2 + side) * quarter, quarter),
            ],
            axis=0,
        )

    def whole_rows(mine):
        theirs = across(mine)
        return jnp.where(
            side == 0,
            jnp.concatenate([mine[:quarter], theirs, mine[quarter:]], axis=0),
            jnp.concatenate([theirs[:quarter], mine, theirs[quarter:]], axis=0),
        )

    one = (lengths[0] > 0).astype(jnp.float32)
    query_theirs = fetch(w_query, one)
    output_theirs = fetch(w_output, one)
    gate_theirs = fetch(w_gate, one)
    up_theirs = fetch(w_up, one)
    down_theirs = fetch(w_down, one)

    used, position = layout(lengths, holder, device, tok_rows)
    cosine, sine = rotary_tables(position)
    row_ids = jnp.arange(tok_rows, dtype=jnp.int32)
    rows = own(row_ids[:, None])
    lows = own((row_ids - position)[:, None])
    cosine_own, sine_own = own(cosine), own(sine)
    valid = own(used.astype(jnp.float32)[:, None])

    normed_all = norm_forward(tokens.astype(jnp.float32), gain_input)[0].astype(jnp.bfloat16)
    key_pre = dot(normed_all, w_key)
    value_states = dot(normed_all, w_value).astype(jnp.bfloat16)
    key_states = rotate(norm_forward(key_pre, gain_key)[0], cosine, sine).astype(jnp.bfloat16)
    _, key_plain, key_inverse = norm_forward(own(key_pre), gain_key)

    source = own(tokens).astype(jnp.float32)
    normed, normed_plain, normed_inverse = norm_forward(source, gain_input)
    normed_low = normed.astype(jnp.bfloat16)
    w_query_all = jnp.concatenate([w_query, query_theirs], axis=1)
    heads = w_query_all.shape[1] // HD
    query_pre = dot(normed_low, w_query_all)
    query_parts, query_norms = [], []
    for h in range(heads):
        out, plain, inverse = norm_forward(query_pre[:, h * HD : (h + 1) * HD], gain_query)
        query_norms.append((plain, inverse))
        query_parts.append(rotate(out, cosine_own, sine_own).astype(jnp.bfloat16))
    queries = jnp.concatenate(query_parts, axis=1)
    spans = ((slice(0, quarter), half_rows), (slice(quarter, half_rows), tok_rows))
    mixed = jnp.concatenate(
        [
            attend(rows[s], lows[s], queries[s], key_states, value_states, key_rows)
            for s, key_rows in spans
        ],
        axis=0,
    )
    w_output_all = jnp.concatenate([w_output, output_theirs], axis=0)
    branch = dot(mixed, w_output_all)
    post_attn, post_attn_plain, post_attn_inverse = norm_forward(branch, gain_post_attn)
    middle = source + post_attn
    normed2, normed2_plain, normed2_inverse = norm_forward(middle, gain_pre_ffn)
    normed2_low = normed2.astype(jnp.bfloat16)
    w_gate_all = jnp.concatenate([w_gate, gate_theirs], axis=1)
    w_up_all = jnp.concatenate([w_up, up_theirs], axis=1)
    w_down_all = jnp.concatenate([w_down, down_theirs], axis=0)
    gate_proj = dot(normed2_low, w_gate_all)
    up_proj = dot(normed2_low, w_up_all)
    activation, gelu_pull = jax.vjp(gelu_tanh, gate_proj)
    hidden = (activation * up_proj).astype(jnp.bfloat16)
    ffn_sum = dot(hidden, w_down_all)
    post_ffn, post_ffn_plain, post_ffn_inverse = norm_forward(ffn_sum, gain_post_ffn)
    layer_out = whole_rows(middle + post_ffn)

    upstream = own(out_grad).astype(jnp.float32) * valid
    grad_ffn, grad_post_ffn = norm_backward(
        upstream, post_ffn_plain, post_ffn_inverse, gain_post_ffn
    )
    grad_ffn_low = grad_ffn.astype(jnp.bfloat16)
    inner = hidden.shape[1] // 2
    down_sum = scatter_sum(
        left_dot(hidden[:, :inner], grad_ffn_low), left_dot(hidden[:, inner:], grad_ffn_low)
    )
    grad_hidden = right_dot(grad_ffn_low, w_down_all)
    grad_gate_low = gelu_pull(grad_hidden * up_proj)[0].astype(jnp.bfloat16)
    grad_up_low = (grad_hidden * activation).astype(jnp.bfloat16)
    gate_sum = scatter_sum(
        left_dot(normed2_low, grad_gate_low[:, :inner]),
        left_dot(normed2_low, grad_gate_low[:, inner:]),
    )
    up_sum = scatter_sum(
        left_dot(normed2_low, grad_up_low[:, :inner]),
        left_dot(normed2_low, grad_up_low[:, inner:]),
    )
    grad_normed2 = right_dot(grad_gate_low, w_gate_all) + right_dot(grad_up_low, w_up_all)
    grad_pre_part, grad_pre_ffn = norm_backward(
        grad_normed2, normed2_plain, normed2_inverse, gain_pre_ffn
    )
    grad_middle = upstream + grad_pre_part
    grad_branch, grad_post_attn = norm_backward(
        grad_middle, post_attn_plain, post_attn_inverse, gain_post_attn
    )
    grad_branch_low = grad_branch.astype(jnp.bfloat16)
    mixed_width = w_output.shape[0]
    output_sum = scatter_sum(
        left_dot(mixed[:, :mixed_width], grad_branch_low),
        left_dot(mixed[:, mixed_width:], grad_branch_low),
    )
    grad_mixed = right_dot(grad_branch_low, w_output_all).astype(jnp.bfloat16)

    (query_early, key_early, value_early), (query_late, key_late, value_late) = [
        attend_back(
            rows[s], lows[s], queries[s], key_states, value_states, grad_mixed[s], key_rows
        )
        for s, key_rows in spans
    ]
    grad_queries = jnp.concatenate([query_early, query_late], axis=0)
    sums = jnp.concatenate([key_late, value_late], axis=1)
    sums = jnp.concatenate(
        [sums[:half_rows] + jnp.concatenate([key_early, value_early], axis=1), sums[half_rows:]],
        axis=0,
    )
    keyvalue = own(sums) + across(others(sums))
    grad_keys, grad_values = keyvalue[:, :HD], keyvalue[:, HD:]

    query_grads, grad_gain_query = [], jnp.zeros((HD,), jnp.float32)
    for h in range(heads):
        plain, inverse = query_norms[h]
        out, gain_part = norm_backward(
            unrotate(grad_queries[:, h * HD : (h + 1) * HD], cosine_own, sine_own),
            plain,
            inverse,
            gain_query,
        )
        query_grads.append(out.astype(jnp.bfloat16))
        grad_gain_query = grad_gain_query + gain_part
    grad_query_low = jnp.concatenate(query_grads, axis=1)
    query_width = w_query.shape[1]
    query_sum = scatter_sum(
        left_dot(normed_low, grad_query_low[:, :query_width]),
        left_dot(normed_low, grad_query_low[:, query_width:]),
    )
    grad_key_pre, grad_gain_key = norm_backward(
        unrotate(grad_keys, cosine_own, sine_own), key_plain, key_inverse, gain_key
    )
    grad_key_low = grad_key_pre.astype(jnp.bfloat16)
    grad_value_low = grad_values.astype(jnp.bfloat16)
    grad_normed = (
        right_dot(grad_query_low, w_query_all)
        + right_dot(grad_key_low, w_key)
        + right_dot(grad_value_low, w_value)
    )
    grad_input_part, grad_gain_input = norm_backward(
        grad_normed, normed_plain, normed_inverse, gain_input
    )
    tokens_grad = whole_rows(grad_middle + grad_input_part)

    gains = (
        grad_gain_input,
        grad_gain_query,
        grad_gain_key,
        grad_post_attn,
        grad_pre_ffn,
        grad_post_ffn,
    )
    packed = jnp.concatenate(gains)
    size = lax.axis_size("dp")
    extra = -(-packed.shape[0] // (HD * size)) * size
    packed = jnp.pad(packed, (0, extra * HD - packed.shape[0])).reshape(extra, HD)
    with_keys = jnp.concatenate([left_dot(normed_low, grad_key_low), packed], axis=0)
    with_values = jnp.concatenate(
        [left_dot(normed_low, grad_value_low), jnp.zeros_like(packed)], axis=0
    )
    pair_sum = scatter_sum(
        jnp.where(side == 0, with_keys, with_values), jnp.where(side == 0, with_values, with_keys)
    )
    pair_other = across(pair_sum)
    pair = jnp.where(
        side == 0,
        jnp.concatenate([pair_sum, pair_other], axis=1),
        jnp.concatenate([pair_other, pair_sum], axis=1),
    )
    pair = spread(pair)
    gain_sums = pair[width:, :HD].reshape(-1)
    gain_outs, at = [], 0
    for gain in gains:
        gain_outs.append(gain_sums[at : at + gain.shape[0]])
        at += gain.shape[0]
    return (
        layer_out,
        tokens_grad,
        spread(query_sum),
        pair[:width, :HD],
        pair[:width, HD:],
        spread(output_sum),
        spread(gate_sum),
        spread(up_sum),
        spread(down_sum),
        *gain_outs,
    )


def solution(mesh):
    return jax.shard_map(
        local,
        mesh=mesh,
        in_specs=(
            P("dp", None),
            P(None, "tensor"),
            P(),
            P(),
            P("tensor", None),
            P(None, "tensor"),
            P(None, "tensor"),
            P("tensor", None),
            P(),
            P(),
            P(),
            P(),
            P(),
            P(),
            P("dp", None),
            P(),
            P(),
        ),
        out_specs=(
            P("dp", None),
            P("dp", None),
            P(None, "tensor"),
            P(),
            P(),
            P("tensor", None),
            P(None, "tensor"),
            P(None, "tensor"),
            P("tensor", None),
            P(),
            P(),
            P(),
            P(),
            P(),
            P(),
        ),
        check_vma=False,
    )
```

```python
import jax
import jax.numpy as jnp
from jax import lax
from jax.experimental import pallas as pl
from jax.experimental.pallas import tpu as pltpu
from jax.sharding import PartitionSpec as P

HD = 256


EPS = 1e-06
THETA = 1000000.0


def layout(lengths, holder, device, tok_rows):
    seq_count = lengths.shape[0]
    owned_mask = holder == device
    local_len = jnp.where(owned_mask, lengths, 0)
    ids = jnp.arange(seq_count, dtype=jnp.int32)
    starts = jnp.sum(jnp.where(ids[:, None] < ids[None, :], local_len[:, None], 0), axis=0)
    row_ids = jnp.arange(tok_rows, dtype=jnp.int32)[:, None]
    inside = (
        owned_mask[None, :]
        & (row_ids >= starts[None, :])
        & (row_ids < (starts + local_len)[None, :])
    )
    reached = jnp.sum(jnp.where(inside, row_ids - starts[None, :] + 1, 0), axis=1)
    return (reached > 0, jnp.maximum(reached - 1, 0))


def rotary_tables(position):
    half_width = HD // 2
    frequency = THETA ** (-(2.0 * jnp.arange(half_width, dtype=jnp.float32)) / HD)
    angles = position.astype(jnp.float32)[:, None] * frequency[None, :]
    return (jnp.cos(angles), jnp.sin(angles))


def rotate(vectors, cosine, sine):
    half_width = HD // 2
    first, second = vectors[:, :half_width], vectors[:, half_width:]
    return jnp.concatenate(
        [first * cosine - second * sine, second * cosine + first * sine], axis=1
    )


def unrotate(grads_in, cosine, sine):
    half_width = HD // 2
    first, second = grads_in[:, :half_width], grads_in[:, half_width:]
    return jnp.concatenate(
        [first * cosine + second * sine, second * cosine - first * sine], axis=1
    )


def norm_forward(vectors, scaling):
    inverse = lax.rsqrt(jnp.mean(vectors * vectors, axis=-1, keepdims=True) + EPS)
    plain = vectors * inverse
    return (plain * (1.0 + scaling), plain, inverse)


def norm_backward(grads_in, plain, inverse, scaling):
    scaled = grads_in * (1.0 + scaling)
    grads_out = inverse * (scaled - plain * jnp.mean(scaled * plain, axis=-1, keepdims=True))
    gain_grad = jnp.sum(grads_in * plain, axis=0)
    return (grads_out, gain_grad)


def dot(first, second):
    return jnp.dot(first, second, preferred_element_type=jnp.float32)


def left_dot(first, second):
    return lax.dot_general(
        first, second, (((0,), (0,)), ((), ())), preferred_element_type=jnp.float32
    )


def right_dot(first, second):
    return lax.dot_general(
        first, second, (((1,), (1,)), ((), ())), preferred_element_type=jnp.float32
    )


def gelu_tanh(vectors):
    return jax.nn.gelu(vectors, approximate=True)


def softmax_rows(row_ref, low_ref, query, keys):
    scores = right_dot(query, keys) * (HD ** (-0.5))
    column_ids = lax.broadcasted_iota(jnp.int32, scores.shape, 1)
    allowed = (column_ids <= row_ref[...]) & (column_ids >= low_ref[...])
    scores = jnp.where(allowed, scores, -1e30)
    exponent = jnp.exp(scores - jnp.max(scores, axis=1, keepdims=True))
    return exponent * (1.0 / jnp.sum(exponent, axis=1, keepdims=True))


def attend_kernel(row_ref, low_ref, query_ref, key_ref, value_ref, mixed_ref):
    probs = softmax_rows(row_ref, low_ref, query_ref[...], key_ref[...])
    mixed_ref[...] = dot(probs.astype(jnp.bfloat16), value_ref[...]).astype(jnp.bfloat16)


def attend_back_kernel(
    row_ref, low_ref, query_ref, key_ref, value_ref, grad_ref, query_grad_ref, key_sum, value_sum
):
    @pl.when(pl.program_id(0) == 0)
    def _():
        key_sum[...] = jnp.zeros_like(key_sum)
        value_sum[...] = jnp.zeros_like(value_sum)

    query, keys, grads_in = query_ref[...], key_ref[...], grad_ref[...]
    probs = softmax_rows(row_ref, low_ref, query, keys)
    value_sum[...] += left_dot(probs.astype(jnp.bfloat16), grads_in)
    grad_probs = right_dot(grads_in, value_ref[...])
    inner = jnp.sum(probs * grad_probs, axis=1, keepdims=True)
    grad_scores = (probs * (grad_probs - inner) * (HD ** (-0.5))).astype(jnp.bfloat16)
    query_grad_ref[...] = dot(grad_scores, keys)
    key_sum[...] += left_dot(grad_scores, query)


def attention_specs(block_rows, key_rows):
    column = pl.BlockSpec((block_rows, 1), lambda h: (0, 0))
    head = pl.BlockSpec((block_rows, HD), lambda h: (0, h))
    keys = pl.BlockSpec((key_rows, HD), lambda h: (0, 0))
    return column, head, keys


def attend(rows, lows, queries, keys, values, key_rows):
    block_rows, width = queries.shape
    heads = width // HD
    column, head, whole = attention_specs(block_rows, key_rows)
    work = block_rows * key_rows * heads
    return pl.pallas_call(
        attend_kernel,
        grid=(heads,),
        out_shape=jax.ShapeDtypeStruct(queries.shape, jnp.bfloat16),
        in_specs=[column, column, head, whole, whole],
        out_specs=head,
        compiler_params=pltpu.CompilerParams(vmem_limit_bytes=40 * 2**20),
        cost_estimate=pl.CostEstimate(
            flops=4 * work * HD, bytes_accessed=4 * 2**20, transcendentals=work
        ),
    )(rows, lows, queries, keys, values)


def attend_back(rows, lows, queries, keys, values, grads_in, key_rows):
    block_rows, width = queries.shape
    heads = width // HD
    column, head, whole = attention_specs(block_rows, key_rows)
    work = block_rows * key_rows * heads
    sums = jax.ShapeDtypeStruct((key_rows, HD), jnp.float32)
    return pl.pallas_call(
        attend_back_kernel,
        grid=(heads,),
        out_shape=(jax.ShapeDtypeStruct(queries.shape, jnp.float32), sums, sums),
        in_specs=[column, column, head, whole, whole, head],
        out_specs=(head, whole, whole),
        compiler_params=pltpu.CompilerParams(vmem_limit_bytes=48 * 2**20),
        cost_estimate=pl.CostEstimate(
            flops=10 * work * HD, bytes_accessed=8 * 2**20, transcendentals=work
        ),
    )(rows, lows, queries, keys, values, grads_in)


def across(array):
    return lax.ppermute(array, "tensor", [(0, 1), (1, 0)])


def swap(array, mask):
    size = lax.axis_size("dp")
    return lax.ppermute(array, "dp", [(i, i ^ mask) for i in range(size)])


def bit_of(mask):
    return (lax.axis_index("dp") // mask) % 2


def halve(array, mask, axis):
    half = array.shape[axis] // 2
    bit = bit_of(mask)
    sent = lax.dynamic_slice_in_dim(array, (1 - bit) * half, half, axis)
    kept = lax.dynamic_slice_in_dim(array, bit * half, half, axis)
    return kept + swap(sent, mask)


def join(array, mask):
    other = swap(array, mask)
    return jnp.where(
        bit_of(mask) == 0,
        jnp.concatenate([array, other], axis=0),
        jnp.concatenate([other, array], axis=0),
    )


def outer_masks(first):
    size = lax.axis_size("dp")
    masks, mask = [], 2
    while mask < size:
        masks.append(mask)
        mask *= 2
    return sorted(masks, key=lambda m: (m != first, m))


def scatter_sum(array, first, axis):
    masks = outer_masks(first)
    array = halve(array, masks[0], axis)
    if axis == 0:
        inner = array.shape[1] // 2
        mine, theirs = array[:, :inner], array[:, inner:]
    else:
        mine, theirs = array[0], array[1]
    total = mine + across(theirs)
    for mask in masks[1:]:
        total = halve(total, mask, 0)
    return total


def spread(total, first):
    for mask in reversed(outer_masks(first)):
        total = join(total, mask)
    return join(total, 1)


def fetch(weight, one, mask):
    quarter = weight.shape[0] // 4
    at = (bit_of(1) * 2 + bit_of(mask)) * quarter
    part = lax.dynamic_slice_in_dim(weight, at, quarter).astype(jnp.float32)
    theirs = join(join(across(part * one), mask), 1)
    return (theirs * one).astype(jnp.bfloat16)


def local(
    tokens,
    w_query,
    w_key,
    w_value,
    w_output,
    w_gate,
    w_up,
    w_down,
    gain_input,
    gain_query,
    gain_key,
    gain_post_attn,
    gain_pre_ffn,
    gain_post_ffn,
    out_grad,
    lengths,
    holder,
):
    tok_rows, width = tokens.shape
    quarter = tok_rows // 4
    half_rows = tok_rows // 2
    device = lax.axis_index("dp")
    side = lax.axis_index("tensor")
    early, late = side * quarter, (3 - side) * quarter

    def own(array):
        return jnp.concatenate(
            [
                lax.dynamic_slice_in_dim(array, early, quarter),
                lax.dynamic_slice_in_dim(array, late, quarter),
            ],
            axis=0,
        )

    def others(array):
        return jnp.concatenate(
            [
                lax.dynamic_slice_in_dim(array, (1 - side) * quarter, quarter),
                lax.dynamic_slice_in_dim(array, (2 + side) * quarter, quarter),
            ],
            axis=0,
        )

    def whole_rows(mine):
        theirs = across(mine)
        return jnp.where(
            side == 0,
            jnp.concatenate([mine[:quarter], theirs, mine[quarter:]], axis=0),
            jnp.concatenate([theirs[:quarter], mine, theirs[quarter:]], axis=0),
        )

    one = (lengths[0] > 0).astype(jnp.float32)
    query_theirs = fetch(w_query, one, 2)
    output_theirs = fetch(w_output, one, 4)
    gate_theirs = fetch(w_gate, one, 2)
    up_theirs = fetch(w_up, one, 4)
    down_theirs = fetch(w_down, one, 2)

    used, position = layout(lengths, holder, device, tok_rows)
    cosine, sine = rotary_tables(position)
    row_ids = jnp.arange(tok_rows, dtype=jnp.int32)
    rows = own(row_ids[:, None])
    lows = own((row_ids - position)[:, None])
    cosine_own, sine_own = own(cosine), own(sine)
    valid = own(used.astype(jnp.float32)[:, None])

    normed_all = norm_forward(tokens.astype(jnp.float32), gain_input)[0].astype(jnp.bfloat16)
    key_pre = dot(normed_all, w_key)
    value_states = dot(normed_all, w_value).astype(jnp.bfloat16)
    key_states = rotate(norm_forward(key_pre, gain_key)[0], cosine, sine).astype(jnp.bfloat16)
    _, key_plain, key_inverse = norm_forward(own(key_pre), gain_key)

    source = own(tokens).astype(jnp.float32)
    normed, normed_plain, normed_inverse = norm_forward(source, gain_input)
    normed_low = normed.astype(jnp.bfloat16)
    w_query_all = jnp.concatenate([w_query, query_theirs], axis=1)
    heads = w_query_all.shape[1] // HD
    query_pre = dot(normed_low, w_query_all)
    query_parts, query_norms = [], []
    for h in range(heads):
        out, plain, inverse = norm_forward(query_pre[:, h * HD : (h + 1) * HD], gain_query)
        query_norms.append((plain, inverse))
        query_parts.append(rotate(out, cosine_own, sine_own).astype(jnp.bfloat16))
    queries = jnp.concatenate(query_parts, axis=1)
    spans = ((slice(0, quarter), half_rows), (slice(quarter, half_rows), tok_rows))
    mixed = jnp.concatenate(
        [
            attend(rows[s], lows[s], queries[s], key_states, value_states, key_rows)
            for s, key_rows in spans
        ],
        axis=0,
    )
    w_output_all = jnp.concatenate([w_output, output_theirs], axis=0)
    branch = dot(mixed, w_output_all)
    post_attn, post_attn_plain, post_attn_inverse = norm_forward(branch, gain_post_attn)
    middle = source + post_attn
    normed2, normed2_plain, normed2_inverse = norm_forward(middle, gain_pre_ffn)
    normed2_low = normed2.astype(jnp.bfloat16)
    w_gate_all = jnp.concatenate([w_gate, gate_theirs], axis=1)
    w_up_all = jnp.concatenate([w_up, up_theirs], axis=1)
    w_down_all = jnp.concatenate([w_down, down_theirs], axis=0)
    gate_proj = dot(normed2_low, w_gate_all)
    up_proj = dot(normed2_low, w_up_all)
    activation, gelu_pull = jax.vjp(gelu_tanh, gate_proj)
    hidden = (activation * up_proj).astype(jnp.bfloat16)
    ffn_sum = dot(hidden, w_down_all)
    post_ffn, post_ffn_plain, post_ffn_inverse = norm_forward(ffn_sum, gain_post_ffn)
    layer_out = whole_rows(middle + post_ffn)

    upstream = own(out_grad).astype(jnp.float32) * valid
    grad_ffn, grad_post_ffn = norm_backward(
        upstream, post_ffn_plain, post_ffn_inverse, gain_post_ffn
    )
    grad_ffn_low = grad_ffn.astype(jnp.bfloat16)
    grad_down = left_dot(hidden, grad_ffn_low).reshape(2, -1, width)
    grad_hidden = right_dot(grad_ffn_low, w_down_all)
    grad_gate_low = gelu_pull(grad_hidden * up_proj)[0].astype(jnp.bfloat16)
    grad_up_low = (grad_hidden * activation).astype(jnp.bfloat16)
    grad_gate = halve(left_dot(normed2_low, grad_gate_low), 1, 0)
    grad_up = halve(left_dot(normed2_low, grad_up_low), 1, 0)
    grad_normed2 = right_dot(grad_gate_low, w_gate_all) + right_dot(grad_up_low, w_up_all)
    grad_pre_part, grad_pre_ffn = norm_backward(
        grad_normed2, normed2_plain, normed2_inverse, gain_pre_ffn
    )
    grad_middle = upstream + grad_pre_part
    grad_branch, grad_post_attn = norm_backward(
        grad_middle, post_attn_plain, post_attn_inverse, gain_post_attn
    )
    grad_branch_low = grad_branch.astype(jnp.bfloat16)
    grad_output = left_dot(mixed, grad_branch_low).reshape(2, -1, width)
    grad_rows = jnp.concatenate([grad_down, grad_output], axis=1)
    grad_mixed = right_dot(grad_branch_low, w_output_all).astype(jnp.bfloat16)
    grad_mixed, grad_gate, grad_up, grad_rows = lax.optimization_barrier(
        (grad_mixed, grad_gate, grad_up, grad_rows)
    )
    gate_sum = scatter_sum(grad_gate, 2, 0)
    up_sum = scatter_sum(grad_up, 4, 0)
    rows_sum = scatter_sum(halve(grad_rows, 1, 1), 4, 1)

    (query_early, key_early, value_early), (query_late, key_late, value_late) = [
        attend_back(
            rows[s], lows[s], queries[s], key_states, value_states, grad_mixed[s], key_rows
        )
        for s, key_rows in spans
    ]
    grad_queries = jnp.concatenate([query_early, query_late], axis=0)
    sums = jnp.concatenate([key_late, value_late], axis=1)
    sums = jnp.concatenate(
        [sums[:half_rows] + jnp.concatenate([key_early, value_early], axis=1), sums[half_rows:]],
        axis=0,
    )
    keyvalue = own(sums) + across(others(sums))
    grad_keys, grad_values = keyvalue[:, :HD], keyvalue[:, HD:]

    query_grads, grad_gain_query = [], jnp.zeros((HD,), jnp.float32)
    for h in range(heads):
        plain, inverse = query_norms[h]
        out, gain_part = norm_backward(
            unrotate(grad_queries[:, h * HD : (h + 1) * HD], cosine_own, sine_own),
            plain,
            inverse,
            gain_query,
        )
        query_grads.append(out.astype(jnp.bfloat16))
        grad_gain_query = grad_gain_query + gain_part
    grad_query_low = jnp.concatenate(query_grads, axis=1)
    query_width = w_query.shape[1]
    grad_key_pre, grad_gain_key = norm_backward(
        unrotate(grad_keys, cosine_own, sine_own), key_plain, key_inverse, gain_key
    )
    grad_key_low = grad_key_pre.astype(jnp.bfloat16)
    grad_value_low = grad_values.astype(jnp.bfloat16)
    grad_normed = (
        right_dot(grad_query_low, w_query_all)
        + right_dot(grad_key_low, w_key)
        + right_dot(grad_value_low, w_value)
    )
    grad_input_part, grad_gain_input = norm_backward(
        grad_normed, normed_plain, normed_inverse, gain_input
    )
    tokens_grad = whole_rows(grad_middle + grad_input_part)

    gains = (
        grad_gain_input,
        grad_gain_query,
        grad_gain_key,
        grad_post_attn,
        grad_pre_ffn,
        grad_post_ffn,
    )
    packed = jnp.concatenate(gains)
    size = lax.axis_size("dp")
    extra = -(-packed.shape[0] // (HD * size)) * size
    packed = jnp.pad(packed, (0, extra * HD - packed.shape[0])).reshape(extra, HD)
    left = side == 0
    columns = jnp.concatenate(
        [
            grad_query_low[:, :query_width],
            jnp.where(left, grad_key_low, grad_value_low),
            grad_query_low[:, query_width:],
            jnp.where(left, grad_value_low, grad_key_low),
        ],
        axis=1,
    )
    empty = jnp.zeros((extra, query_width), jnp.float32)
    below = jnp.concatenate(
        [empty, jnp.where(left, packed, 0.0), empty, jnp.where(left, 0.0, packed)], axis=1
    )
    grad_columns = jnp.concatenate([left_dot(normed_low, columns), below], axis=0)
    columns_sum = scatter_sum(halve(grad_columns, 1, 0), 2, 0)
    pair_sum = columns_sum[:, query_width:]
    pair_other = across(pair_sum)
    columns_out = spread(
        jnp.concatenate(
            [
                columns_sum[:, :query_width],
                jnp.where(left, pair_sum, pair_other),
                jnp.where(left, pair_other, pair_sum),
            ],
            axis=1,
        ),
        2,
    )
    gain_sums = columns_out[width:, query_width : query_width + HD].reshape(-1)
    gain_outs, at = [], 0
    for gain in gains:
        gain_outs.append(gain_sums[at : at + gain.shape[0]])
        at += gain.shape[0]
    grad_rows_out = spread(rows_sum, 4)
    down_rows = w_down.shape[0]
    return (
        layer_out,
        tokens_grad,
        columns_out[:width, :query_width],
        columns_out[:width, query_width : query_width + HD],
        columns_out[:width, query_width + HD :],
        grad_rows_out[down_rows:],
        spread(gate_sum, 2),
        spread(up_sum, 4),
        grad_rows_out[:down_rows],
        *gain_outs,
    )


def solution(mesh):
    return jax.shard_map(
        local,
        mesh=mesh,
        in_specs=(
            P("dp", None),
            P(None, "tensor"),
            P(),
            P(),
            P("tensor", None),
            P(None, "tensor"),
            P(None, "tensor"),
            P("tensor", None),
            P(),
            P(),
            P(),
            P(),
            P(),
            P(),
            P("dp", None),
            P(),
            P(),
        ),
        out_specs=(
            P("dp", None),
            P("dp", None),
            P(None, "tensor"),
            P(),
            P(),
            P("tensor", None),
            P(None, "tensor"),
            P(None, "tensor"),
            P("tensor", None),
            P(),
            P(),
            P(),
            P(),
            P(),
            P(),
        ),
        check_vma=False,
    )
```
